32 devices in a mesh: tm: 4 (over x, core), tile: 8 (over z, y).
Axes of the slice: x: 2, y: 2, z: 4, core: 2. Of those that a mesh axis runs over, the one named last changes fastest.
Arguments:
- latents: bfloat16 [8, 160, 16, 16], P('tm', 'tile'), may hold values from -6 to 6
- w_in: bfloat16 [3, 3, 3, 16, 384], replicated, may hold values from -0.3125 to 0.3125
- b_in: bfloat16 [384], replicated, may hold values from -3 to 3
- w_up: bfloat16 [3, 3, 384, 192], replicated, may hold values from -0.109375 to 0.109375
- b_up: bfloat16 [192], replicated, may hold values from -3 to 3
- gain_one: bfloat16 [192], replicated, may hold values from 0.099609375 to 1.8984375
- w_one: bfloat16 [3, 3, 3, 192, 192], replicated, may hold values from -0.078125 to 0.078125
- b_one: bfloat16 [192], replicated, may hold values from -3 to 3
- gain_two: bfloat16 [192], replicated, may hold values from 0.099609375 to 1.8984375
- w_two: bfloat16 [3, 3, 3, 192, 192], replicated, may hold values from -0.078125 to 0.078125
- b_two: bfloat16 [192], replicated, may hold values from -3 to 3
Outputs:
- decoded: bfloat16 [8, 32, 320, 192], P('tm', 'tile')
The draws below stay inside these ranges and needn't reach their ends.
All inputs are finite; a program needn't handle non-finite values.
Results may differ from the reference program's by a relative error of at most 0.0095.
Values may be sent and summed in bfloat16 or wider, within the bound.
A program may use at most 64 MiB of HBM per device.

```python
import jax
import jax.numpy as jnp
from jax import lax

ZCH = 16
DIM = 384
UPD = 192
COLS = 160
FRAMES = 8
HEIGHT = 16


def level_of(rng, shape, cuts, low, high):
    factor_of, own = 1.0, jax.random.fold_in(rng, 6)
    for axis_at, blocks in cuts:
        draws = jnp.exp(jax.random.uniform(jax.random.fold_in(own, axis_at), (blocks,), jnp.float32, low / len(cuts), high / len(cuts)))
        factor_of = factor_of * jnp.repeat(draws, shape[axis_at] // blocks).reshape([-1 if axis == axis_at else 1 for axis in range(len(shape))])
    return factor_of


def scatter_about(stream_key, dims, width, reach, split=(), held_as=jnp.bfloat16):
    gain = level_of(stream_key, dims, split, -0.22, 0.18) if split else 1.0
    values = jax.random.normal(stream_key, dims, jnp.float32) * width * gain
    return jnp.minimum(jnp.maximum(values, -reach), reach).astype(held_as)


def setup_inputs(seed: int = 0) -> dict:
    arg_keys = jax.random.split(jax.random.key(seed), 12)
    latents = scatter_about(arg_keys[0], (FRAMES, COLS, HEIGHT, ZCH), 1.0, 6.0, ((0, 4), (1, 8)))
    w_in = scatter_about(arg_keys[1], (3, 3, 3, ZCH, DIM), (27 * ZCH) ** -0.5, 0.3125)
    b_in = scatter_about(arg_keys[2], (DIM,), 0.5, 3.0)
    w_up = scatter_about(arg_keys[3], (3, 3, DIM, UPD), (9 * DIM) ** -0.5, 0.109375)
    b_up = scatter_about(arg_keys[4], (UPD,), 0.5, 3.0)
    gain_one = jnp.clip(1.0 + 0.18 * jax.random.normal(arg_keys[5], (UPD,), jnp.float32), 0.099609375, 1.8984375).astype(jnp.bfloat16)
    w_one = scatter_about(arg_keys[6], (3, 3, 3, UPD, UPD), (27 * UPD) ** -0.5, 0.078125)
    b_one = scatter_about(arg_keys[7], (UPD,), 0.5, 3.0)
    gain_two = jnp.clip(1.0 + 0.18 * jax.random.normal(arg_keys[8], (UPD,), jnp.float32), 0.099609375, 1.8984375).astype(jnp.bfloat16)
    w_two = scatter_about(arg_keys[9], (3, 3, 3, UPD, UPD), (27 * UPD) ** -0.5, 0.078125)
    b_two = scatter_about(arg_keys[10], (UPD,), 0.5, 3.0)
    return {"latents": latents, "w_in": w_in, "b_in": b_in, "w_up": w_up, "b_up": b_up, "gain_one": gain_one, "w_one": w_one, "b_one": b_one, "gain_two": gain_two, "w_two": w_two, "b_two": b_two}


def activate(values_in, gain_vec):
    values_in = values_in.astype(jnp.float32)
    inverse_rms = lax.rsqrt(lax.optimization_barrier(jnp.mean(values_in * values_in, axis=-1, keepdims=True)) + 1e-06)
    return jax.nn.silu(values_in * inverse_rms * gain_vec.astype(jnp.float32)).astype(jnp.bfloat16)

def causal_conv(field_in, kernel, bias_vec):
    padded = jnp.pad(field_in.astype(jnp.float32), ((2, 0), (1, 1), (1, 1), (0, 0)))
    result = lax.conv_general_dilated(padded[None], kernel.astype(jnp.float32), (1, 1, 1), 'VALID', dimension_numbers=('NDHWC', 'DHWIO', 'NDHWC'), precision=lax.Precision.HIGHEST)[0]
    return result + bias_vec.astype(jnp.float32)

def plane_conv(field_in, kernel, bias_vec):
    padded = jnp.pad(field_in.astype(jnp.float32), ((0, 0), (1, 1), (1, 1), (0, 0)))
    result = lax.conv_general_dilated(padded, kernel.astype(jnp.float32), (1, 1), 'VALID', dimension_numbers=('NHWC', 'HWIO', 'NHWC'), precision=lax.Precision.HIGHEST)
    return result + bias_vec.astype(jnp.float32)

def reference(latents, w_in, b_in, w_up, b_up, gain_one, w_one, b_one, gain_two, w_two, b_two):
    latent_grid = jnp.transpose(latents, (0, 2, 1, 3))
    first_out = causal_conv(latent_grid, w_in, b_in).astype(jnp.bfloat16)
    enlarged = jnp.repeat(jnp.repeat(first_out, 2, axis=1), 2, axis=2)
    plane_out = plane_conv(enlarged, w_up, b_up).astype(jnp.bfloat16)
    act_one = activate(plane_out, gain_one)
    middle = causal_conv(act_one, w_one, b_one).astype(jnp.bfloat16)
    act_two = activate(middle, gain_two)
    decoded = plane_out.astype(jnp.float32) + causal_conv(act_two, w_two, b_two)
    return decoded.astype(jnp.bfloat16)
```

```python
import functools

import jax
import jax.numpy as jnp
from jax import lax
from jax.experimental import pallas as pl
from jax.experimental.pallas import tpu as pltpu
from jax.sharding import PartitionSpec as P

MESH = pl.DeviceIdType.MESH
F32 = jnp.float32
BF16 = jnp.bfloat16


def dot(a, b):
    return jnp.dot(a, b, preferred_element_type=F32)


def activate(v, gain):
    v = v.astype(F32)
    inv = lax.rsqrt(jnp.mean(v * v, axis=-1, keepdims=True) + 1e-6)
    half = 0.5 * (v * inv * gain)
    return half + half * jnp.tanh(half)


def after(v):
    rolled = pltpu.roll(v, 1, 0)
    return jnp.where(lax.broadcasted_iota(jnp.int32, v.shape, 0) == 0, 0.0, rolled)


def ahead(v):
    n = v.shape[0]
    rolled = pltpu.roll(v, n - 1, 0)
    return jnp.where(lax.broadcasted_iota(jnp.int32, v.shape, 0) == n - 1, 0.0, rolled)


def kernel(ntm, nt, height, shard, zch,
           lat, w_in, b_in, w_up, b_up, g_one, w_one, b_one, g_two, w_two, b_two,
           out,
           lbuf, lf32, sel, cols, first, wc, plane, a1, a2, acc,
           lsend, lrecv, osend, hsend, arecv):
    tm = lax.axis_index("tm")
    tile = lax.axis_index("tile")
    ncol = nt * shard
    dim = first.shape[-1]
    upd = plane.shape[-1]

    barrier = pltpu.get_barrier_semaphore()

    def others(d, body):
        def step(k, c):
            body(lax.rem(tile + k, nt))
            return c
        lax.fori_loop(1 if d == 0 else 0, nt, step, 0)

    for d in range(3):
        @pl.when(tm - d >= 0)
        def _():
            others(d, lambda s: pl.semaphore_signal(
                barrier, inc=1, device_id=(tm - d, s), device_id_type=MESH))
    pl.semaphore_wait(barrier, nt * jnp.minimum(3, ntm - tm) - 1)

    def send_lat(d, s):
        return pltpu.make_async_remote_copy(
            src_ref=lat, dst_ref=lbuf.at[d, tile], send_sem=lsend.at[d, s],
            recv_sem=lrecv.at[d, tile], device_id=(tm + d, s), device_id_type=MESH)

    for d in (2, 1, 0):
        @pl.when(tm + d < ntm)
        def _():
            others(d, lambda s: send_lat(d, s).start())

    lbuf[0, tile] = lat[...]
    for d in (1, 2):
        @pl.when(tm - d < 0)
        def _():
            lbuf[d] = jnp.zeros(lbuf.shape[1:], BF16)

    wide = height * zch
    for r in range(4):
        k = lax.broadcasted_iota(jnp.int32, (wide, 256), 0)
        n = lax.broadcasted_iota(jnp.int32, (wide, 256), 1)
        krow, kch = k // zch, k % zch
        p, ch = n // (3 * zch), n % zch
        hit = (krow == 2 * tile - 2 + r + p) & (kch == ch) & (n < 9 * zch)
        sel[:, 256 * r:256 * r + 256] = jnp.where(hit, 1.0, 0.0).astype(BF16)

    def phases(j, c):
        at = pl.ds(pl.multiple_of(j * 64, 64), 64)
        w = [[w_up[3 * p + q, at].astype(F32) for q in range(3)] for p in range(3)]

        def joined(v, phase):
            if phase == 0:
                return [v[0], v[1] + v[2]]
            return [v[0] + v[1], v[2]]

        for a in range(2):
            rows = [joined([w[p][q] for p in range(3)], a) for q in range(3)]
            for b in range(2):
                for rr in range(2):
                    both = joined([rows[q][rr] for q in range(3)], b)
                    for cc in range(2):
                        wc[2 * a + b, 2 * rr + cc, at] = both[cc].astype(BF16)
        return c
    lax.fori_loop(0, dim // 64, phases, 0)

    for d in range(3):
        @pl.when(tm - d >= 0)
        def _():
            def arrived(s):
                pltpu.make_async_remote_copy(
                    src_ref=lat, dst_ref=lbuf.at[d, s], send_sem=lsend.at[d, s],
                    recv_sem=lrecv.at[d, s], device_id=(tm, s), device_id_type=MESH).wait_recv()
            others(d, arrived)

    for d in range(3):
        for s in range(nt):
            v = lbuf[d, s].astype(F32)
            for f in range(2):
                lf32[2 * (2 - d) + f, s * shard:(s + 1) * shard] = v[f * shard:(f + 1) * shard]

    def gather(f, c):
        raw = lf32[f].astype(BF16)
        for r in range(4):
            z = dot(raw, sel[:, 256 * r:256 * r + 256])
            q = lax.broadcasted_iota(jnp.int32, z.shape, 1) % (3 * zch) // zch
            z = jnp.where(q == 0, after(z), jnp.where(q == 2, ahead(z), z))
            cols[f, r] = z.astype(BF16)
        return c
    lax.fori_loop(0, 6, gather, 0)

    def conv_in(k, c):
        f, r = k // 4, k % 4
        v = b_in[...] + sum(dot(cols[f + a, r][:, :9 * zch], w_in[a]) for a in range(3))
        row = 2 * tile - 1 + r
        keep = ((row >= 0) & (row < height)).astype(F32)
        v = v * keep
        first[0, f, r] = after(v).astype(BF16)
        first[1, f, r] = v.astype(BF16)
        first[2, f, r] = ahead(v).astype(BF16)
        return c
    lax.fori_loop(0, 16, conv_in, 0)

    def split_store(ref, at, b, v):
        if b == 0:
            ref[at[0], at[1], ncol:2 * ncol] = v.astype(BF16)
            ref[at[0], at[1], 3 * ncol:] = ahead(v).astype(BF16)
        else:
            ref[at[0], at[1], 2 * ncol:3 * ncol] = v.astype(BF16)
            ref[at[0], at[1], :ncol] = after(v).astype(BF16)

    def conv_up(f, c):
        seen = ((tm > 0) | (f >= 2))
        for a in range(2):
            for b in range(2):
                v = b_up[...]
                for rr in range(2):
                    for cc in range(2):
                        x = first[b + cc, f, rr:rr + 3].reshape(3 * ncol, dim)
                        v = v + dot(x, wc[2 * a + b, 2 * rr + cc])
                v = v.astype(BF16)
                for base in range(3):
                    row = 2 * base + 1 - a
                    here = v[base * ncol:(base + 1) * ncol]
                    plane[f, row, b * ncol:(b + 1) * ncol] = here
                    ok = seen
                    if row == 0:
                        ok = ok & (tile > 0)
                    if row == 5:
                        ok = ok & (tile < nt - 1)
                    split_store(a1, (f, row), b, activate(here, g_one[...]) * ok.astype(F32))
        return c
    lax.fori_loop(0, 4, conv_up, 0)

    def conv_part(ref, w, f, r, kts):
        total = None
        for kt in kts:
            for kh in range(3):
                for kw in range(3):
                    x = ref[f + kt, r + kh, kw * ncol:(kw + 2) * ncol]
                    term = dot(x, w[9 * kt + 3 * kh + kw])
                    total = term if total is None else total + term
        return total

    centre = pl.ds(ncol, 2 * ncol)

    def copy(f, row, to_f, to_row, dtm, dtile, send):
        return pltpu.make_async_remote_copy(
            src_ref=a2.at[f, row, centre], dst_ref=a2.at[to_f, to_row, centre], send_sem=send,
            recv_sem=arecv.at[to_f, to_row], device_id=(tm + dtm, tile + dtile),
            device_id_type=MESH)

    def sends(f, r, act):
        @pl.when(tm + 1 < ntm)
        def _():
            act(copy(f + 2, r + 1, f, r + 1, 1, 0, osend.at[f, r]))

        @pl.when((r == 0) & (tile > 0))
        def _():
            act(copy(f + 2, r + 1, f + 2, 5, 0, -1, hsend.at[f, 0, 0]))

        @pl.when((r == 0) & (tile > 0) & (tm + 1 < ntm))
        def _():
            act(copy(f + 2, r + 1, f, 5, 1, -1, hsend.at[f, 0, 1]))

        @pl.when((r == 3) & (tile < nt - 1))
        def _():
            act(copy(f + 2, r + 1, f + 2, 0, 0, 1, hsend.at[f, 1, 0]))

        @pl.when((r == 3) & (tile < nt - 1) & (tm + 1 < ntm))
        def _():
            act(copy(f + 2, r + 1, f, 0, 1, 1, hsend.at[f, 1, 1]))

    def where_at(k):
        f = k % 2
        h = k // 2
        return f, jnp.where(h == 0, 0, jnp.where(h == 1, 3, h - 1))

    def conv_mid(k, c):
        f, r = where_at(k)
        v = (conv_part(a1, w_one, f, r, (0, 1, 2)) + b_one[...]).astype(BF16)
        v = activate(v, g_two[...])
        split_store(a2, (f + 2, r + 1), 0, v[:ncol])
        split_store(a2, (f + 2, r + 1), 1, v[ncol:])
        sends(f, r, lambda c: c.start())
        return c
    lax.fori_loop(0, 8, conv_mid, 0)

    def receive(f, row, ok):
        @pl.when(ok)
        def _():
            copy(f, row, f, row, 0, 0, osend.at[0, 0]).wait_recv()
            a2[f, row, 3 * ncol:] = ahead(a2[f, row, ncol:2 * ncol].astype(F32)).astype(BF16)
            a2[f, row, :ncol] = after(a2[f, row, 2 * ncol:3 * ncol].astype(F32)).astype(BF16)

        @pl.when(jnp.logical_not(ok))
        def _():
            a2[f, row] = jnp.zeros(a2.shape[2:], BF16)

    for f in (2, 3):
        receive(f, 0, tile > 0)
        receive(f, 5, tile < nt - 1)

    def conv_near(r, c):
        acc[0, r] = conv_part(a2, w_two, 0, r, (2,))
        acc[1, r] = conv_part(a2, w_two, 1, r, (1, 2))
        return c
    lax.fori_loop(0, 4, conv_near, 0)

    for f in (0, 1):
        receive(f, 0, (tm > 0) & (tile > 0))
        receive(f, 5, (tm > 0) & (tile < nt - 1))

        def middle_rows(row, c):
            receive(f, row, tm > 0)
            return c
        lax.fori_loop(1, 5, middle_rows, 0)

    m = lax.broadcasted_iota(jnp.int32, (2 * ncol, 2 * ncol), 0)
    n = lax.broadcasted_iota(jnp.int32, (2 * ncol, 2 * ncol), 1)
    weave = jnp.where(n == (m % 2) * ncol + m // 2, 1.0, 0.0).astype(BF16)

    def conv_far(r, c):
        for f, kts in ((0, (0, 1)), (1, (0,))):
            v = acc[f, r] + conv_part(a2, w_two, f, r, kts) + b_two[...]
            v = (v + plane[f + 2, r + 1].astype(F32)).astype(BF16)
            out[f, r] = dot(weave, v).astype(BF16)
        return c
    lax.fori_loop(0, 4, conv_far, 0)

    for d in range(3):
        @pl.when(tm + d < ntm)
        def _():
            others(d, lambda s: send_lat(d, s).wait_send())

    def left(k, c):
        f, r = where_at(k)
        sends(f, r, lambda c: c.wait_send())
        return c
    lax.fori_loop(0, 8, left, 0)


def per_device(latents, w_in, b_in, w_up, b_up, gain_one, w_one, b_one, gain_two, w_two, b_two):
    ntm, nt = lax.axis_size("tm"), lax.axis_size("tile")
    frames, shard, height, zch = latents.shape
    dim, upd = w_up.shape[2:]
    ncol = nt * shard
    lat = latents.reshape(frames * shard, height * zch)
    deep = -(-frames * shard // 16) * 16
    lat = jnp.pad(lat, ((0, deep - frames * shard), (0, 0)))
    wide = height * zch
    vec = lambda v: v.astype(F32).reshape(1, -1)
    args = (lat, w_in.reshape(3, 9 * zch, dim), vec(b_in), w_up.reshape(9, dim, upd), vec(b_up),
            vec(gain_one), w_one.reshape(27, upd, upd), vec(b_one), vec(gain_two),
            w_two.reshape(27, upd, upd), vec(b_two))
    vmem = pl.BlockSpec(memory_space=pltpu.VMEM)
    dma = pltpu.SemaphoreType.DMA
    return pl.pallas_call(
        functools.partial(kernel, ntm, nt, height, shard, zch),
        out_shape=jax.ShapeDtypeStruct((frames, 4, 2 * ncol, upd), BF16),
        in_specs=[vmem] * len(args),
        out_specs=vmem,
        scratch_shapes=[
            pltpu.VMEM((3, nt, deep, wide), BF16),
            pltpu.VMEM((6, ncol, wide), F32),
            pltpu.VMEM((wide, 1024), BF16),
            pltpu.VMEM((6, 4, ncol, 256), BF16),
            pltpu.VMEM((3, 4, 4, ncol, dim), BF16),
            pltpu.VMEM((4, 4, dim, upd), BF16),
            pltpu.VMEM((4, 6, 2 * ncol, upd), BF16),
            pltpu.VMEM((4, 6, 4 * ncol, upd), BF16),
            pltpu.VMEM((4, 6, 4 * ncol, upd), BF16),
            pltpu.VMEM((2, 4, 2 * ncol, upd), F32),
            dma((3, nt)),
            dma((3, nt)),
            dma((2, 4)),
            dma((2, 2, 2)),
            dma((4, 6)),
        ],
        compiler_params=pltpu.CompilerParams(
            collective_id=0, has_side_effects=True, vmem_limit_bytes=60 * 2**20),
    )(*args)


def solution(mesh):
    placed = (P("tm", "tile", None, None),) + (P(),) * 10
    return jax.shard_map(
        per_device,
        mesh=mesh,
        in_specs=placed,
        out_specs=P("tm", "tile", None, None),
        check_vma=False,
    )
```

```python
import functools

import jax
import jax.numpy as jnp
from jax import lax
from jax.experimental import pallas as pl
from jax.experimental.pallas import tpu as pltpu
from jax.sharding import PartitionSpec as P

MESH = pl.DeviceIdType.MESH
F32 = jnp.float32
BF16 = jnp.bfloat16


def dot(a, b):
    return jnp.dot(a, b, preferred_element_type=F32)


def dot_t(a, b):
    return lax.dot_general(a, b, (((1,), (1,)), ((), ())), preferred_element_type=F32)


def activate(v, gain):
    v = v.astype(F32)
    inv = lax.rsqrt(jnp.mean(v * v, axis=-1, keepdims=True) + 1e-6)
    half = 0.5 * (v * inv * gain)
    return half + half * jnp.tanh(half)


def after(v):
    rolled = pltpu.roll(v, 1, 0)
    return jnp.where(lax.broadcasted_iota(jnp.int32, v.shape, 0) == 0, 0.0, rolled)


def ahead(v):
    n = v.shape[0]
    rolled = pltpu.roll(v, n - 1, 0)
    return jnp.where(lax.broadcasted_iota(jnp.int32, v.shape, 0) == n - 1, 0.0, rolled)


def kernel(ntm, nt, height, shard, zch,
           lat, w_in, w_up, w_one, w_two, vb_in, vb_up, vg_one, vb_one, vg_two, vb_two, out,
           lbuf, lf32, sel, cols, first, wc, plane, a1, a2, acc,
           lsend, lrecv, osend, hsend, arecv):
    tm = lax.axis_index("tm")
    tile = lax.axis_index("tile")
    ncol = nt * shard
    dim = first.shape[-1]
    upd = plane.shape[-1]

    b_in, b_up, g_one, b_one, g_two, b_two = (
        v[...].astype(F32).reshape(1, v.shape[0])
        for v in (vb_in, vb_up, vg_one, vb_one, vg_two, vb_two))

    barrier = pltpu.get_barrier_semaphore()

    def others(d, body):
        def step(k, c):
            body(lax.rem(tile + k, nt))
            return c
        lax.fori_loop(1 if d == 0 else 0, nt, step, 0)

    for d in range(3):
        @pl.when(tm - d >= 0)
        def _():
            others(d, lambda s: pl.semaphore_signal(
                barrier, inc=1, device_id=(tm - d, s), device_id_type=MESH))
    pl.semaphore_wait(barrier, nt * jnp.minimum(3, ntm - tm) - 1)

    def send_lat(d, s):
        return pltpu.make_async_remote_copy(
            src_ref=lat, dst_ref=lbuf.at[d, tile], send_sem=lsend.at[d, s],
            recv_sem=lrecv.at[d, tile], device_id=(tm + d, s), device_id_type=MESH)

    for d in (2, 1, 0):
        @pl.when(tm + d < ntm)
        def _():
            others(d, lambda s: send_lat(d, s).start())

    lbuf[0, tile] = lat[...]
    for d in (1, 2):
        @pl.when(tm - d < 0)
        def _():
            lbuf[d] = jnp.zeros(lbuf.shape[1:], BF16)

    wide = height * zch
    for r in range(4):
        k = lax.broadcasted_iota(jnp.int32, (wide, 256), 0)
        n = lax.broadcasted_iota(jnp.int32, (wide, 256), 1)
        krow, kch = k // zch, k % zch
        p, ch = n // (3 * zch), n % zch
        hit = (krow == 2 * tile - 2 + r + p) & (kch == ch) & (n < 9 * zch)
        sel[:, 256 * r:256 * r + 256] = jnp.where(hit, 1.0, 0.0).astype(BF16)

    def phases(j, c):
        at = pl.ds(pl.multiple_of(j * 32, 32), 32)
        w = [[w_up[3 * p + q, at].astype(F32) for q in range(3)] for p in range(3)]

        def joined(v, phase):
            if phase == 0:
                return [v[0], v[1] + v[2]]
            return [v[0] + v[1], v[2]]

        for a in range(2):
            rows = [joined([w[p][q] for p in range(3)], a) for q in range(3)]
            for b in range(2):
                for rr in range(2):
                    both = joined([rows[q][rr] for q in range(3)], b)
                    for cc in range(2):
                        wc[2 * a + b, 2 * rr + cc, at] = both[cc].astype(BF16)
        return c
    lax.fori_loop(0, upd // 32, phases, 0)

    for d in range(3):
        @pl.when(tm - d >= 0)
        def _():
            def arrived(s):
                pltpu.make_async_remote_copy(
                    src_ref=lat, dst_ref=lbuf.at[d, s], send_sem=lsend.at[d, s],
                    recv_sem=lrecv.at[d, s], device_id=(tm, s), device_id_type=MESH).wait_recv()
            others(d, arrived)

    for d in range(3):
        for s in range(nt):
            v = lbuf[d, s].astype(F32)
            for f in range(2):
                lf32[2 * (2 - d) + f, s * shard:(s + 1) * shard] = v[f * shard:(f + 1) * shard]

    def gather(f, c):
        raw = lf32[f].astype(BF16)
        for r in range(4):
            z = dot(raw, sel[:, 256 * r:256 * r + 256])
            q = lax.broadcasted_iota(jnp.int32, z.shape, 1) % (3 * zch) // zch
            z = jnp.where(q == 0, after(z), jnp.where(q == 2, ahead(z), z))
            cols[f, r] = z.astype(BF16)
        return c
    lax.fori_loop(0, 6, gather, 0)

    def conv_in(k, c):
        f, r = k // 4, k % 4
        v = b_in + sum(dot(cols[f + a, r][:, :9 * zch], w_in[a]) for a in range(3))
        row = 2 * tile - 1 + r
        keep = ((row >= 0) & (row < height)).astype(F32)
        v = v * keep
        first[0, f, r] = after(v).astype(BF16)
        first[1, f, r] = v.astype(BF16)
        first[2, f, r] = ahead(v).astype(BF16)
        return c
    lax.fori_loop(0, 16, conv_in, 0)

    def split_store(ref, at, b, v):
        if b == 0:
            ref[at[0], at[1], ncol:2 * ncol] = v.astype(BF16)
            ref[at[0], at[1], 3 * ncol:] = ahead(v).astype(BF16)
        else:
            ref[at[0], at[1], 2 * ncol:3 * ncol] = v.astype(BF16)
            ref[at[0], at[1], :ncol] = after(v).astype(BF16)

    def conv_up(f, c):
        seen = ((tm > 0) | (f >= 2))
        for a in range(2):
            for b in range(2):
                v = b_up
                for rr in range(2):
                    for cc in range(2):
                        x = first[b + cc, f, rr:rr + 3].reshape(3 * ncol, dim)
                        v = v + dot_t(x, wc[2 * a + b, 2 * rr + cc])
                v = v.astype(BF16)
                for base in range(3):
                    row = 2 * base + 1 - a
                    here = v[base * ncol:(base + 1) * ncol]
                    plane[f, row, b * ncol:(b + 1) * ncol] = here
                    ok = seen
                    if row == 0:
                        ok = ok & (tile > 0)
                    if row == 5:
                        ok = ok & (tile < nt - 1)
                    split_store(a1, (f, row), b, activate(here, g_one) * ok.astype(F32))
        return c
    lax.fori_loop(0, 4, conv_up, 0)

    def conv_part(ref, w, f, r, kts):
        total = None
        for kt in kts:
            for kh in range(3):
                for kw in range(3):
                    x = ref[f + kt, r + kh, kw * ncol:(kw + 2) * ncol]
                    term = dot(x, w[9 * kt + 3 * kh + kw])
                    total = term if total is None else total + term
        return total

    centre = pl.ds(ncol, 2 * ncol)

    def copy(f, row, to_f, to_row, dtm, dtile, send):
        return pltpu.make_async_remote_copy(
            src_ref=a2.at[f, row, centre], dst_ref=a2.at[to_f, to_row, centre], send_sem=send,
            recv_sem=arecv.at[to_f, to_row], device_id=(tm + dtm, tile + dtile),
            device_id_type=MESH)

    def sends(f, r, act):
        @pl.when(tm + 1 < ntm)
        def _():
            act(copy(f + 2, r + 1, f, r + 1, 1, 0, osend.at[f, r]))

        @pl.when((r == 0) & (tile > 0))
        def _():
            act(copy(f + 2, r + 1, f + 2, 5, 0, -1, hsend.at[f, 0, 0]))

        @pl.when((r == 3) & (tile < nt - 1))
        def _():
            act(copy(f + 2, r + 1, f + 2, 0, 0, 1, hsend.at[f, 1, 0]))

    def forwards(f, act):
        @pl.when((tm > 0) & (tile > 0))
        def _():
            act(copy(f, 1, f, 5, 0, -1, hsend.at[f, 0, 1]))

        @pl.when((tm > 0) & (tile < nt - 1))
        def _():
            act(copy(f, 4, f, 0, 0, 1, hsend.at[f, 1, 1]))

    def where_at(k):
        f = k % 2
        h = k // 2
        return f, jnp.where(h == 0, 0, jnp.where(h == 1, 3, h - 1))

    def conv_mid(k, c):
        f, r = where_at(k)
        v = (conv_part(a1, w_one, f, r, (0, 1, 2)) + b_one).astype(BF16)
        v = activate(v, g_two)
        split_store(a2, (f + 2, r + 1), 0, v[:ncol])
        split_store(a2, (f + 2, r + 1), 1, v[ncol:])
        sends(f, r, lambda c: c.start())
        return c
    lax.fori_loop(0, 8, conv_mid, 0)

    for f in (0, 1):
        @pl.when(tm > 0)
        def _():
            for row in (1, 4):
                copy(f, row, f, row, 0, 0, osend.at[0, 0]).wait_recv()
        forwards(f, lambda c: c.start())

    def receive(f, row, ok, wait=True):
        @pl.when(ok)
        def _():
            if wait:
                copy(f, row, f, row, 0, 0, osend.at[0, 0]).wait_recv()
            a2[f, row, 3 * ncol:] = ahead(a2[f, row, ncol:2 * ncol].astype(F32)).astype(BF16)
            a2[f, row, :ncol] = after(a2[f, row, 2 * ncol:3 * ncol].astype(F32)).astype(BF16)

        @pl.when(jnp.logical_not(ok))
        def _():
            a2[f, row] = jnp.zeros(a2.shape[2:], BF16)

    for f in (2, 3):
        receive(f, 0, tile > 0)
        receive(f, 5, tile < nt - 1)

    def conv_near(r, c):
        acc[0, r] = conv_part(a2, w_two, 0, r, (2,))
        acc[1, r] = conv_part(a2, w_two, 1, r, (1, 2))
        return c
    lax.fori_loop(0, 4, conv_near, 0)

    for f in (0, 1):
        for row in (1, 2, 3, 4):
            receive(f, row, tm > 0, row in (2, 3))
        receive(f, 0, (tm > 0) & (tile > 0))
        receive(f, 5, (tm > 0) & (tile < nt - 1))

    m = lax.broadcasted_iota(jnp.int32, (2 * ncol, 2 * ncol), 0)
    n = lax.broadcasted_iota(jnp.int32, (2 * ncol, 2 * ncol), 1)
    weave = jnp.where(m == (n % 2) * ncol + n // 2, 1.0, 0.0).astype(BF16)

    def conv_far(r, c):
        for f, kts in ((0, (0, 1)), (1, (0,))):
            v = acc[f, r] + conv_part(a2, w_two, f, r, kts) + b_two
            v = (v + plane[f + 2, r + 1].astype(F32)).astype(BF16)
            out[f, r] = lax.dot_general(
                v, weave, (((0,), (0,)), ((), ())), preferred_element_type=F32).astype(BF16)
        return c
    lax.fori_loop(0, 4, conv_far, 0)

    for d in range(3):
        @pl.when(tm + d < ntm)
        def _():
            others(d, lambda s: send_lat(d, s).wait_send())

    def left(k, c):
        f, r = where_at(k)
        sends(f, r, lambda c: c.wait_send())
        return c
    lax.fori_loop(0, 8, left, 0)
    for f in (0, 1):
        forwards(f, lambda c: c.wait_send())


def per_device(latents, w_in, b_in, w_up, b_up, gain_one, w_one, b_one, gain_two, w_two, b_two):
    ntm, nt = lax.axis_size("tm"), lax.axis_size("tile")
    frames, shard, height, zch = latents.shape
    dim, upd = w_up.shape[2:]
    ncol = nt * shard
    lat = latents.reshape(frames * shard, height * zch)
    deep = -(-frames * shard // 16) * 16
    lat = jnp.pad(lat, ((0, deep - frames * shard), (0, 0)))
    wide = height * zch
    args = (lat, w_in.reshape(3, 9 * zch, dim),
            jnp.swapaxes(w_up, 2, 3).reshape(9, upd, dim), w_one.reshape(27, upd, upd),
            w_two.reshape(27, upd, upd), b_in, b_up, gain_one, b_one, gain_two, b_two)
    vmem = pl.BlockSpec(memory_space=pltpu.VMEM)
    dma = pltpu.SemaphoreType.DMA
    decoded = pl.pallas_call(
        functools.partial(kernel, ntm, nt, height, shard, zch),
        out_shape=jax.ShapeDtypeStruct((frames, 4, upd, 2 * ncol), BF16),
        in_specs=[vmem] * len(args),
        out_specs=vmem,
        scratch_shapes=[
            pltpu.VMEM((3, nt, deep, wide), BF16),
            pltpu.VMEM((6, ncol, wide), F32),
            pltpu.VMEM((wide, 1024), BF16),
            pltpu.VMEM((6, 4, ncol, 256), BF16),
            pltpu.VMEM((3, 4, 4, ncol, dim), BF16),
            pltpu.VMEM((4, 4, upd, dim), BF16),
            pltpu.VMEM((4, 6, 2 * ncol, upd), BF16),
            pltpu.VMEM((4, 6, 4 * ncol, upd), BF16),
            pltpu.VMEM((4, 6, 4 * ncol, upd), BF16),
            pltpu.VMEM((2, 4, 2 * ncol, upd), F32),
            dma((3, nt)),
            dma((3, nt)),
            dma((2, 4)),
            dma((2, 2, 2)),
            dma((4, 6)),
        ],
        compiler_params=pltpu.CompilerParams(
            collective_id=0, has_side_effects=True, vmem_limit_bytes=60 * 2**20),
    )(*args)
    return jnp.swapaxes(decoded, 2, 3)


def solution(mesh):
    placed = (P("tm", "tile", None, None),) + (P(),) * 10
    return jax.shard_map(
        per_device,
        mesh=mesh,
        in_specs=placed,
        out_specs=P("tm", "tile", None, None),
        check_vma=False,
    )
```

```python
import functools

import jax
import jax.numpy as jnp
from jax import lax
from jax.experimental import pallas as pl
from jax.experimental.pallas import tpu as pltpu
from jax.sharding import PartitionSpec as P

MESH = pl.DeviceIdType.MESH
F32 = jnp.float32
BF16 = jnp.bfloat16


def dot(a, b):
    return jnp.dot(a, b, preferred_element_type=F32)


def dot_t(a, b):
    return lax.dot_general(a, b, (((1,), (1,)), ((), ())), preferred_element_type=F32)


def activate(v, gain):
    v = v.astype(F32)
    inv = lax.rsqrt(jnp.mean(v * v, axis=-1, keepdims=True) + 1e-6)
    half = 0.5 * (v * inv * gain)
    return half + half * jnp.tanh(half)


def after(v):
    rolled = pltpu.roll(v, 1, 0)
    return jnp.where(lax.broadcasted_iota(jnp.int32, v.shape, 0) == 0, 0.0, rolled)


def ahead(v):
    n = v.shape[0]
    rolled = pltpu.roll(v, n - 1, 0)
    return jnp.where(lax.broadcasted_iota(jnp.int32, v.shape, 0) == n - 1, 0.0, rolled)


def kernel(ntm, nt, height, shard, zch,
           lat, w_in, w_up, far_one, far_two, vb_in, vb_up, vg_one, vb_one, vg_two, vb_two, out,
           lbuf, lf32, sel, cols, first, wc, plane, a1, a2, acc,
           lsend, lrecv, osend, hsend, arecv, w_one, w_two, wsem):
    tm = lax.axis_index("tm")
    tile = lax.axis_index("tile")
    ncol = nt * shard
    dim = first.shape[-1]
    upd = plane.shape[-1]

    b_in, b_up, g_one, b_one, g_two, b_two = (
        v[...].astype(F32).reshape(1, v.shape[0])
        for v in (vb_in, vb_up, vg_one, vb_one, vg_two, vb_two))

    fetch_one = pltpu.make_async_copy(far_one, w_one, wsem.at[0])
    fetch_two = pltpu.make_async_copy(far_two, w_two, wsem.at[1])
    fetch_one.start()
    fetch_two.start()

    barrier = pltpu.get_barrier_semaphore()

    def others(d, body):
        def step(k, c):
            body(lax.rem(tile + k, nt))
            return c
        lax.fori_loop(1 if d == 0 else 0, nt, step, 0)

    for d in range(3):
        @pl.when(tm - d >= 0)
        def _():
            others(d, lambda s: pl.semaphore_signal(
                barrier, inc=1, device_id=(tm - d, s), device_id_type=MESH))
    pl.semaphore_wait(barrier, nt * jnp.minimum(3, ntm - tm) - 1)

    def send_lat(d, s):
        return pltpu.make_async_remote_copy(
            src_ref=lat, dst_ref=lbuf.at[d, tile], send_sem=lsend.at[d, s],
            recv_sem=lrecv.at[d, tile], device_id=(tm + d, s), device_id_type=MESH)

    for d in (2, 1, 0):
        @pl.when(tm + d < ntm)
        def _():
            others(d, lambda s: send_lat(d, s).start())

    lbuf[0, tile] = lat[...]
    for d in (1, 2):
        @pl.when(tm - d < 0)
        def _():
            lbuf[d] = jnp.zeros(lbuf.shape[1:], BF16)

    wide = height * zch
    for r in range(4):
        k = lax.broadcasted_iota(jnp.int32, (wide, 256), 0)
        n = lax.broadcasted_iota(jnp.int32, (wide, 256), 1)
        krow, kch = k // zch, k % zch
        p, ch = n // (3 * zch), n % zch
        hit = (krow == 2 * tile - 2 + r + p) & (kch == ch) & (n < 9 * zch)
        sel[:, 256 * r:256 * r + 256] = jnp.where(hit, 1.0, 0.0).astype(BF16)

    def phases(j, c):
        at = pl.ds(pl.multiple_of(j * 32, 32), 32)
        w = [[w_up[3 * p + q, at].astype(F32) for q in range(3)] for p in range(3)]

        def joined(v, phase):
            if phase == 0:
                return [v[0], v[1] + v[2]]
            return [v[0] + v[1], v[2]]

        for a in range(2):
            rows = [joined([w[p][q] for p in range(3)], a) for q in range(3)]
            for b in range(2):
                for rr in range(2):
                    both = joined([rows[q][rr] for q in range(3)], b)
                    for cc in range(2):
                        wc[2 * a + b, 2 * rr + cc, at] = both[cc].astype(BF16)
        return c
    lax.fori_loop(0, upd // 32, phases, 0)

    for d in range(3):
        @pl.when(tm - d >= 0)
        def _():
            def arrived(s):
                pltpu.make_async_remote_copy(
                    src_ref=lat, dst_ref=lbuf.at[d, s], send_sem=lsend.at[d, s],
                    recv_sem=lrecv.at[d, s], device_id=(tm, s), device_id_type=MESH).wait_recv()
            others(d, arrived)

    for d in range(3):
        for s in range(nt):
            v = lbuf[d, s].astype(F32)
            for f in range(2):
                lf32[2 * (2 - d) + f, s * shard:(s + 1) * shard] = v[f * shard:(f + 1) * shard]

    def gather(f, c):
        raw = lf32[f].astype(BF16)
        for r in range(4):
            z = dot(raw, sel[:, 256 * r:256 * r + 256])
            q = lax.broadcasted_iota(jnp.int32, z.shape, 1) % (3 * zch) // zch
            z = jnp.where(q == 0, after(z), jnp.where(q == 2, ahead(z), z))
            cols[f, r] = z.astype(BF16)
        return c
    lax.fori_loop(0, 6, gather, 0)

    def conv_in(k, c):
        f, r = k // 4, k % 4
        v = b_in + sum(dot(cols[f + a, r][:, :9 * zch], w_in[a]) for a in range(3))
        row = 2 * tile - 1 + r
        keep = ((row >= 0) & (row < height)).astype(F32)
        v = v * keep
        first[0, f, r] = after(v).astype(BF16)
        first[1, f, r] = v.astype(BF16)
        first[2, f, r] = ahead(v).astype(BF16)
        return c
    lax.fori_loop(0, 16, conv_in, 0)

    def split_store(ref, at, b, v):
        if b == 0:
            ref[at[0], at[1], ncol:2 * ncol] = v.astype(BF16)
            ref[at[0], at[1], 3 * ncol:] = ahead(v).astype(BF16)
        else:
            ref[at[0], at[1], 2 * ncol:3 * ncol] = v.astype(BF16)
            ref[at[0], at[1], :ncol] = after(v).astype(BF16)

    def conv_up(f, c):
        seen = ((tm > 0) | (f >= 2))
        for a in range(2):
            for b in range(2):
                v = b_up
                for rr in range(2):
                    for cc in range(2):
                        x = first[b + cc, f, rr:rr + 3].reshape(3 * ncol, dim)
                        v = v + dot_t(x, wc[2 * a + b, 2 * rr + cc])
                v = v.astype(BF16)
                for base in range(3):
                    row = 2 * base + 1 - a
                    here = v[base * ncol:(base + 1) * ncol]
                    plane[f, row, b * ncol:(b + 1) * ncol] = here
                    ok = seen
                    if row == 0:
                        ok = ok & (tile > 0)
                    if row == 5:
                        ok = ok & (tile < nt - 1)
                    split_store(a1, (f, row), b, activate(here, g_one) * ok.astype(F32))
        return c
    lax.fori_loop(0, 4, conv_up, 0)

    def conv_part(ref, w, f, r, kts):
        total = None
        for kt in kts:
            for kh in range(3):
                for kw in range(3):
                    x = ref[f + kt, r + kh, kw * ncol:(kw + 2) * ncol]
                    term = dot(x, w[9 * kt + 3 * kh + kw])
                    total = term if total is None else total + term
        return total

    centre = pl.ds(ncol, 2 * ncol)

    def copy(f, row, to_f, to_row, dtm, dtile, send):
        return pltpu.make_async_remote_copy(
            src_ref=a2.at[f, row, centre], dst_ref=a2.at[to_f, to_row, centre], send_sem=send,
            recv_sem=arecv.at[to_f, to_row], device_id=(tm + dtm, tile + dtile),
            device_id_type=MESH)

    def sends(f, r, act):
        @pl.when(tm + 1 < ntm)
        def _():
            act(copy(f + 2, r + 1, f, r + 1, 1, 0, osend.at[f, r]))

        @pl.when((r == 0) & (tile > 0))
        def _():
            act(copy(f + 2, r + 1, f + 2, 5, 0, -1, hsend.at[f, 0, 0]))

        @pl.when((r == 3) & (tile < nt - 1))
        def _():
            act(copy(f + 2, r + 1, f + 2, 0, 0, 1, hsend.at[f, 1, 0]))

    def forwards(f, act):
        @pl.when((tm > 0) & (tile > 0))
        def _():
            act(copy(f, 1, f, 5, 0, -1, hsend.at[f, 0, 1]))

        @pl.when((tm > 0) & (tile < nt - 1))
        def _():
            act(copy(f, 4, f, 0, 0, 1, hsend.at[f, 1, 1]))

    def where_at(k):
        f = k % 2
        h = k // 2
        return f, jnp.where(h == 0, 0, jnp.where(h == 1, 3, h - 1))

    def conv_mid(k, c):
        f, r = where_at(k)
        v = (conv_part(a1, w_one, f, r, (0, 1, 2)) + b_one).astype(BF16)
        v = activate(v, g_two)
        split_store(a2, (f + 2, r + 1), 0, v[:ncol])
        split_store(a2, (f + 2, r + 1), 1, v[ncol:])
        sends(f, r, lambda c: c.start())
        return c
    fetch_one.wait()
    fetch_two.wait()
    lax.fori_loop(0, 8, conv_mid, 0)

    for f in (0, 1):
        @pl.when(tm > 0)
        def _():
            for row in (1, 4):
                copy(f, row, f, row, 0, 0, osend.at[0, 0]).wait_recv()
        forwards(f, lambda c: c.start())

    def receive(f, row, ok, wait=True):
        @pl.when(ok)
        def _():
            if wait:
                copy(f, row, f, row, 0, 0, osend.at[0, 0]).wait_recv()
            a2[f, row, 3 * ncol:] = ahead(a2[f, row, ncol:2 * ncol].astype(F32)).astype(BF16)
            a2[f, row, :ncol] = after(a2[f, row, 2 * ncol:3 * ncol].astype(F32)).astype(BF16)

        @pl.when(jnp.logical_not(ok))
        def _():
            a2[f, row] = jnp.zeros(a2.shape[2:], BF16)

    for f in (2, 3):
        receive(f, 0, tile > 0)
        receive(f, 5, tile < nt - 1)

    def conv_near(r, c):
        acc[0, r] = conv_part(a2, w_two, 0, r, (2,))
        acc[1, r] = conv_part(a2, w_two, 1, r, (1, 2))
        return c
    lax.fori_loop(0, 4, conv_near, 0)

    for f in (0, 1):
        for row in (1, 2, 3, 4):
            receive(f, row, tm > 0, row in (2, 3))
        receive(f, 0, (tm > 0) & (tile > 0))
        receive(f, 5, (tm > 0) & (tile < nt - 1))

    m = lax.broadcasted_iota(jnp.int32, (2 * ncol, 2 * ncol), 0)
    n = lax.broadcasted_iota(jnp.int32, (2 * ncol, 2 * ncol), 1)
    weave = jnp.where(m == (n % 2) * ncol + n // 2, 1.0, 0.0).astype(BF16)

    def conv_far(r, c):
        for f, kts in ((0, (0, 1)), (1, (0,))):
            v = acc[f, r] + conv_part(a2, w_two, f, r, kts) + b_two
            v = (v + plane[f + 2, r + 1].astype(F32)).astype(BF16)
            out[f, r] = lax.dot_general(
                v, weave, (((0,), (0,)), ((), ())), preferred_element_type=F32).astype(BF16)
        return c
    lax.fori_loop(0, 4, conv_far, 0)

    for d in range(3):
        @pl.when(tm + d < ntm)
        def _():
            others(d, lambda s: send_lat(d, s).wait_send())

    def left(k, c):
        f, r = where_at(k)
        sends(f, r, lambda c: c.wait_send())
        return c
    lax.fori_loop(0, 8, left, 0)
    for f in (0, 1):
        forwards(f, lambda c: c.wait_send())


def per_device(latents, w_in, b_in, w_up, b_up, gain_one, w_one, b_one, gain_two, w_two, b_two):
    ntm, nt = lax.axis_size("tm"), lax.axis_size("tile")
    frames, shard, height, zch = latents.shape
    dim, upd = w_up.shape[2:]
    ncol = nt * shard
    lat = latents.reshape(frames * shard, height * zch)
    deep = -(-frames * shard // 16) * 16
    lat = jnp.pad(lat, ((0, deep - frames * shard), (0, 0)))
    wide = height * zch
    args = (lat, w_in.reshape(3, 9 * zch, dim),
            jnp.swapaxes(w_up, 2, 3).reshape(9, upd, dim), w_one.reshape(27, upd, upd),
            w_two.reshape(27, upd, upd), b_in, b_up, gain_one, b_one, gain_two, b_two)
    vmem = pl.BlockSpec(memory_space=pltpu.VMEM)
    dma = pltpu.SemaphoreType.DMA
    decoded = pl.pallas_call(
        functools.partial(kernel, ntm, nt, height, shard, zch),
        out_shape=jax.ShapeDtypeStruct((frames, 4, upd, 2 * ncol), BF16),
        in_specs=[vmem] * 3 + [pl.BlockSpec(memory_space=pl.ANY)] * 2 + [vmem] * 6,
        out_specs=vmem,
        scratch_shapes=[
            pltpu.VMEM((3, nt, deep, wide), BF16),
            pltpu.VMEM((6, ncol, wide), F32),
            pltpu.VMEM((wide, 1024), BF16),
            pltpu.VMEM((6, 4, ncol, 256), BF16),
            pltpu.VMEM((3, 4, 4, ncol, dim), BF16),
            pltpu.VMEM((4, 4, upd, dim), BF16),
            pltpu.VMEM((4, 6, 2 * ncol, upd), BF16),
            pltpu.VMEM((4, 6, 4 * ncol, upd), BF16),
            pltpu.VMEM((4, 6, 4 * ncol, upd), BF16),
            pltpu.VMEM((2, 4, 2 * ncol, upd), F32),
            dma((3, nt)),
            dma((3, nt)),
            dma((2, 4)),
            dma((2, 2, 2)),
            dma((4, 6)),
            pltpu.VMEM((27, upd, upd), BF16),
            pltpu.VMEM((27, upd, upd), BF16),
            dma((2,)),
        ],
        compiler_params=pltpu.CompilerParams(
            collective_id=0, has_side_effects=True, vmem_limit_bytes=60 * 2**20),
    )(*args)
    return jnp.swapaxes(decoded, 2, 3)


def solution(mesh):
    placed = (P("tm", "tile", None, None),) + (P(),) * 10
    return jax.shard_map(
        per_device,
        mesh=mesh,
        in_specs=placed,
        out_specs=P("tm", "tile", None, None),
        check_vma=False,
    )
```
